32 devices in a mesh: groups: 2 (over y), row: 4 (over x, core), col: 4 (over z).
Axes of the slice: x: 2, y: 2, z: 4, core: 2. Of those that a mesh axis runs over, the one named last changes fastest.
Arguments:
- features: bfloat16 [512, 256, 128], P(('groups', 'row'), 'col'), parts along dimension 0, may hold values from -6 to 6
- kernel_first: bfloat16 [3, 3, 128, 128], replicated, may hold values from -0.1875 to 0.1875
- bias_first: float32 [128], replicated, may hold values from -3 to 3
- mixer_first: bfloat16 [128, 128], replicated, may hold values from -0.5 to 0.5
- shift_first: float32 [128], replicated, may hold values from -3 to 3
- kernel_second: bfloat16 [3, 3, 128, 128], replicated, may hold values from -0.1875 to 0.1875
- bias_second: float32 [128], replicated, may hold values from -3 to 3
- mixer_second: bfloat16 [128, 128], replicated, may hold values from -0.5 to 0.5
- shift_second: float32 [128], replicated, may hold values from -3 to 3
Outputs:
- contacts: float32 [512, 256, 128], P(('groups', 'row'), 'col'), parts along dimension 0
The draws below stay inside these ranges and needn't reach their ends.
There are 2 independent parts, one for each index of `groups`. The reference program is written for one: setup_inputs(seed, part) draws one part's arguments, and reference() takes and returns one part's arrays. A program takes and returns all parts, laid end to end along the dimension named above; an argument that names none is the same for every part. Nothing has to cross between parts.
All inputs are finite; a program needn't handle non-finite values.
Results may differ from the reference program's by a relative error of at most 0.0045.
Values may be sent and summed in bfloat16 or wider, within the bound.
A program may use at most 64 MiB of HBM per device.

```python
import jax
import jax.numpy as jnp

C = 128
L = 256


def block_scale(stream_key, shape, shards, smallest, high):
    def one(position, blocks):
        heights = jax.random.uniform(jax.random.fold_in(jax.random.fold_in(stream_key, 6), position), (blocks,), jnp.float32, smallest / len(shards), high / len(shards))
        return jnp.repeat(jnp.exp(heights), shape[position] // blocks).reshape((-1,) + (1,) * (len(shape) - position - 1))

    gain = one(*shards[0])
    for cut in shards[1:]:
        gain = gain * one(*cut)
    return gain


def noise(key, dims, width, reach, cuts=(), kind=jnp.bfloat16):
    values = width * jax.random.normal(key, dims, jnp.float32)
    if cuts:
        values = values * block_scale(key, dims, cuts, -0.22, 0.18)
    return jnp.clip(values, -reach, reach).astype(kind)


def setup_inputs(seed: int = 0, part: int = 0) -> dict:
    key_list = jax.random.split(jax.random.key(seed), 10)
    own_keys = jax.random.split(jax.random.fold_in(key_list[9], part), 10)
    features = noise(own_keys[0], (L, L, C), 1.0, 6.0, ((0, 4), (1, 4)))
    kernel_first = noise(key_list[1], (3, 3, C, C), (9 * C) ** -0.5, 0.1875)
    bias_first = noise(key_list[2], (C,), 0.5, 3.0, (), jnp.float32)
    mixer_first = noise(key_list[3], (C, C), C ** -0.5, 0.5)
    shift_first = noise(key_list[4], (C,), 0.5, 3.0, (), jnp.float32)
    kernel_second = noise(key_list[5], (3, 3, C, C), (9 * C) ** -0.5, 0.1875)
    bias_second = noise(key_list[6], (C,), 0.5, 3.0, (), jnp.float32)
    mixer_second = noise(key_list[7], (C, C), C ** -0.5, 0.5)
    shift_second = noise(key_list[8], (C,), 0.5, 3.0, (), jnp.float32)
    return {"features": features, "kernel_first": kernel_first, "bias_first": bias_first, "mixer_first": mixer_first, "shift_first": shift_first, "kernel_second": kernel_second, "bias_second": bias_second, "mixer_second": mixer_second, "shift_second": shift_second}


def run_block(source, kernel, conv_bias, mixer, mix_bias, spread):
    extent = source.shape[0]
    channels = source.shape[2]
    padded = jnp.pad(source, ((spread, spread), (spread, spread), (0, 0)))
    total = jnp.zeros((extent * extent, channels), jnp.float32)
    for tap_row in range(3):
        for tap_col in range(3):
            window = padded[tap_row * spread:tap_row * spread + extent, tap_col * spread:tap_col * spread + extent, :]
            total = total + jnp.dot(window.reshape(extent * extent, channels), kernel[tap_row, tap_col], preferred_element_type=jnp.float32)
    activated = jax.nn.relu(total + conv_bias).astype(jnp.bfloat16)
    mixed = jnp.dot(activated, mixer, preferred_element_type=jnp.float32) + mix_bias
    summed = (source.reshape(extent * extent, channels).astype(jnp.float32) + mixed).astype(jnp.bfloat16)
    summed = summed.reshape(extent, extent, channels).astype(jnp.float32)
    return jax.nn.relu((summed + jnp.swapaxes(summed, 0, 1)) * 0.5)


def reference(features, kernel_first, bias_first, mixer_first, shift_first, kernel_second, bias_second, mixer_second, shift_second):
    first = run_block(features, kernel_first, bias_first, mixer_first, shift_first, 2).astype(jnp.bfloat16)
    return run_block(first, kernel_second, bias_second, mixer_second, shift_second, 4)
```

```python
import functools

import jax
import jax.numpy as jnp
from jax import lax
from jax.experimental import pallas as pl
from jax.experimental.pallas import tpu as pltpu
from jax.sharding import PartitionSpec as P

MESH = pl.DeviceIdType.MESH
FIRST, SECOND = 2, 4
BLOCK = 16


def pack(edge, at, width):
    per = 8 // width
    rows, _, channels = edge.shape
    parts = edge.reshape(rows // per, per, 8, channels)
    lane = lax.broadcasted_iota(jnp.int32, (rows // per, 8, channels), 1)
    packed = None
    for m in range(per):
        shift = (m * width - at) % 8
        part = parts[:, m]
        part = pltpu.roll(part, shift, 1) if shift else part
        packed = part if m == 0 else jnp.where(lane >= m * width, part, packed)
    return packed.reshape(rows * width, channels).astype(jnp.bfloat16)


def unpack(packed, at, width):
    per = 8 // width
    tiles = packed.shape[0] // 8
    channels = packed.shape[1]
    packed = packed.astype(jnp.float32).reshape(tiles, 8, channels)
    parts = []
    for m in range(per):
        shift = (at - m * width) % 8
        parts.append(pltpu.roll(packed, shift, 1) if shift else packed)
    return jnp.stack(parts, axis=1).reshape(tiles * per, 8, channels)


def patch(shifted, spread, lo, rows, left, right):
    extent = shifted.shape[2]
    channels = shifted.shape[3]
    lane = lax.broadcasted_iota(jnp.int32, (rows, 16, channels), 1)
    at = pl.ds(spread + lo, rows)
    strip = unpack(left, 0, spread)
    old = shifted[0, at, 0:16, :].astype(jnp.float32)
    new = jnp.where(lane < spread, jnp.concatenate([strip, strip], axis=1), old)
    shifted[0, at, 0:16, :] = new.astype(jnp.bfloat16)
    strip = unpack(right, 8 - spread, spread)
    old = shifted[2, at, extent - 16 : extent, :].astype(jnp.float32)
    new = jnp.where(lane >= 16 - spread, jnp.concatenate([strip, strip], axis=1), old)
    shifted[2, at, extent - 16 : extent, :] = new.astype(jnp.bfloat16)


def kernel(
    x, k1, b1, m1, s1, k2, b2, m2, s2, out,
    xs1, xs2, h, mir, flip, w2, so1, si1, so2, si2,
    strip_send, strip_recv, rows_send, rows_recv, mir_send, mir_recv,
):
    extent, _, channels = x.shape
    chunks = extent // BLOCK
    order = [0] + [chunks - 1] * (chunks > 1) + list(range(1, chunks - 1))
    r, c = lax.axis_index("row"), lax.axis_index("col")
    nr, nc = lax.axis_size("row"), lax.axis_size("col")
    has_up, has_down, has_left, has_right = r > 0, r < nr - 1, c > 0, c < nc - 1
    up, down = {"row": r - 1}, {"row": r + 1}
    left, right = {"col": c - 1}, {"col": c + 1}
    mirror = {"row": c, "col": r}
    off = r != c

    barrier = pltpu.get_barrier_semaphore()
    peers = ((has_up, up), (has_down, down), (has_left, left), (has_right, right), (off, mirror))
    for has, peer in peers:
        @pl.when(has)
        def _():
            pl.semaphore_signal(barrier, inc=1, device_id=peer, device_id_type=MESH)
    count = sum(has.astype(jnp.int32) for has, _ in peers)

    so1[0] = pack(x[:, 0:16, :].astype(jnp.float32)[:, 0:8], 0, FIRST)
    so1[1] = pack(x[:, extent - 16 : extent, :].astype(jnp.float32)[:, 8:16], 8 - FIRST, FIRST)
    pl.semaphore_wait(barrier, count)

    def strips(src, dst, n):
        return (
            (has_left, pltpu.make_async_remote_copy(
                src.at[0], dst.at[1], strip_send.at[n, 0], strip_recv.at[n, 1],
                device_id=left, device_id_type=MESH)),
            (has_right, pltpu.make_async_remote_copy(
                src.at[1], dst.at[0], strip_send.at[n, 1], strip_recv.at[n, 0],
                device_id=right, device_id_type=MESH)),
        )

    def start(copies):
        for has, copy in copies:
            @pl.when(has)
            def _():
                copy.start()

    def finish_strips(copies, dst):
        (hl, to_left), (hr, to_right) = copies

        @pl.when(hl)
        def _():
            to_left.wait_send()
            to_right.wait_recv()

        @pl.when(hr)
        def _():
            to_right.wait_send()
            to_left.wait_recv()

        @pl.when(jnp.logical_not(hl))
        def _():
            dst[0] = jnp.zeros(dst.shape[1:], dst.dtype)

        @pl.when(jnp.logical_not(hr))
        def _():
            dst[1] = jnp.zeros(dst.shape[1:], dst.dtype)

    def halo_rows(shifted, spread, n):
        return (
            (has_up, pltpu.make_async_remote_copy(
                shifted.at[:, spread : 2 * spread], shifted.at[:, extent + spread : extent + 2 * spread],
                rows_send.at[n, 0], rows_recv.at[n, 1], device_id=up, device_id_type=MESH)),
            (has_down, pltpu.make_async_remote_copy(
                shifted.at[:, extent : extent + spread], shifted.at[:, 0:spread],
                rows_send.at[n, 1], rows_recv.at[n, 0], device_id=down, device_id_type=MESH)),
        )

    def finish_rows(copies, shifted, spread):
        (hu, to_up), (hd, to_down) = copies
        zeros = jnp.zeros((3, spread) + shifted.shape[2:], shifted.dtype)

        @pl.when(hu)
        def _():
            to_up.wait_send()
            to_down.wait_recv()

        @pl.when(hd)
        def _():
            to_down.wait_send()
            to_up.wait_recv()

        @pl.when(jnp.logical_not(hu))
        def _():
            shifted[:, 0:spread] = zeros

        @pl.when(jnp.logical_not(hd))
        def _():
            shifted[:, extent + spread : extent + 2 * spread] = zeros

    def spread_rows(shifted, spread, at, cells):
        shifted[1, at] = cells.astype(jnp.bfloat16)
        shifted[0, at] = pltpu.roll(cells, spread, 1).astype(jnp.bfloat16)
        shifted[2, at] = pltpu.roll(cells, extent - spread, 1).astype(jnp.bfloat16)

    first_strips = strips(so1, si1, 0)
    start(first_strips)

    @pl.loop(0, extent // 4)
    def _(step):
        spread_rows(xs1, FIRST, pl.ds(FIRST + step * 4, 4), x[pl.ds(step * 4, 4)].astype(jnp.float32))

    finish_strips(first_strips, si1)

    for k in range(chunks):
        n = BLOCK * FIRST
        patch(xs1, FIRST, k * BLOCK, BLOCK, si1[0, k * n : (k + 1) * n], si1[1, k * n : (k + 1) * n])

    first_rows = halo_rows(xs1, FIRST, 0)
    start(first_rows)
    for p in range(3):
        for q in range(3):
            at = pl.ds((p * 3 + q) * channels, channels)
            w2[at, 0:channels] = k2[at, :]
            w2[at, channels : 2 * channels] = k2[pl.ds((q * 3 + p) * channels, channels), :]
    finish_rows(first_rows, xs1, FIRST)

    def mirror_copy(k):
        cut = pl.ds(k * BLOCK, BLOCK)
        return pltpu.make_async_remote_copy(
            h.at[:, cut], mir.at[:, cut], mir_send.at[k], mir_recv.at[k],
            device_id=mirror, device_id_type=MESH)

    def local_copy(k):
        cut = pl.ds(k * BLOCK, BLOCK)
        return pltpu.make_async_copy(h.at[:, cut], mir.at[:, cut], mir_send.at[k])

    for k in order:
        cut = slice(k * BLOCK, (k + 1) * BLOCK)

        @pl.loop(0, extent // BLOCK)
        def _(step):
            row = step * BLOCK
            taps = [
                xs1[q, pl.ds(row + p * FIRST, BLOCK), cut, :].reshape(BLOCK * BLOCK, channels)
                for p in range(3)
                for q in range(3)
            ]
            total = jnp.dot(jnp.concatenate(taps, axis=1), k1[...], preferred_element_type=jnp.float32)
            acted = jnp.maximum(total + b1[...], 0.0).astype(jnp.bfloat16)
            mixed = jnp.dot(acted, m1[...], preferred_element_type=jnp.float32) + s1[...]
            summed = (taps[4].astype(jnp.float32) + mixed).astype(jnp.bfloat16)
            h[pl.ds(row, BLOCK), cut, :] = summed.reshape(BLOCK, BLOCK, channels)

        @pl.when(off)
        def _():
            mirror_copy(k).start()

        @pl.when(jnp.logical_not(off))
        def _():
            local_copy(k).start()

    second_rows = halo_rows(xs2, SECOND, 1)

    def finish_chunk(k):
        copies = strips(so2.at[k], si2.at[k], 1 + k)
        finish_strips(copies, si2.at[k])
        patch(xs2, SECOND, k * BLOCK, BLOCK, si2[k, 0], si2[k, 1])
        if k == 0:
            start(second_rows[:1])
        if k == chunks - 1:
            start(second_rows[1:])

    for n, k in enumerate(order):
        cut = slice(k * BLOCK, (k + 1) * BLOCK)

        @pl.when(off)
        def _():
            mirror_copy(k).wait()

        @pl.when(jnp.logical_not(off))
        def _():
            local_copy(k).wait()

        flip[...] = mir[:, cut, :].astype(jnp.float32).reshape(extent * BLOCK, channels)
        for b in range(BLOCK):
            other = flip[pl.ds(b, extent, stride=BLOCK), :]
            row = k * BLOCK + b
            mean = jnp.maximum((h[row].astype(jnp.float32) + other) * 0.5, 0.0)
            spread_rows(xs2, SECOND, pl.ds(SECOND + row, 1), mean.reshape(1, extent, channels))
        at = pl.ds(SECOND + k * BLOCK, BLOCK)
        so2[k, 0] = pack(xs2[1, at, 0:16, :].astype(jnp.float32)[:, 0:8], 0, SECOND)
        so2[k, 1] = pack(
            xs2[1, at, extent - 16 : extent, :].astype(jnp.float32)[:, 8:16], 8 - SECOND, SECOND)
        start(strips(so2.at[k], si2.at[k], 1 + k))
        if n:
            finish_chunk(order[n - 1])
    finish_chunk(order[-1])
    finish_rows(second_rows, xs2, SECOND)

    group = 4

    @pl.loop(0, extent // group)
    def _(step):
        row = step * group
        taps = [
            xs2[q, pl.ds(row + p * SECOND, group)].reshape(group * extent, channels)
            for p in range(3)
            for q in range(3)
        ]
        total = jnp.dot(jnp.concatenate(taps, axis=1), w2[...], preferred_element_type=jnp.float32)
        center = taps[4].astype(jnp.float32)
        halves = []
        for side in range(2):
            part = total[:, side * channels : (side + 1) * channels]
            acted = jnp.maximum(part + b2[...], 0.0).astype(jnp.bfloat16)
            mixed = jnp.dot(acted, m2[...], preferred_element_type=jnp.float32) + s2[...]
            halves.append((center + mixed).astype(jnp.bfloat16).astype(jnp.float32))
        mean = jnp.maximum((halves[0] + halves[1]) * 0.5, 0.0)
        out[pl.ds(row, group)] = mean.reshape(group, extent, channels)


def body(
    features,
    kernel_first,
    bias_first,
    mixer_first,
    shift_first,
    kernel_second,
    bias_second,
    mixer_second,
    shift_second,
):
    extent, _, channels = features.shape
    chunks = extent // BLOCK
    bf16 = jnp.bfloat16
    cells = extent * extent
    vmem = pl.BlockSpec(memory_space=pltpu.VMEM)
    return pl.pallas_call(
        kernel,
        out_shape=jax.ShapeDtypeStruct(features.shape, jnp.float32),
        in_specs=[vmem] * 9,
        out_specs=vmem,
        scratch_shapes=[
            pltpu.VMEM((3, extent + 2 * FIRST, extent, channels), bf16),
            pltpu.VMEM((3, extent + 2 * SECOND, extent, channels), bf16),
            pltpu.VMEM((extent, extent, channels), bf16),
            pltpu.VMEM((extent, extent, channels), bf16),
            pltpu.VMEM((extent * BLOCK, channels), jnp.float32),
            pltpu.VMEM((9 * channels, 2 * channels), bf16),
            pltpu.VMEM((2, extent * FIRST, channels), bf16),
            pltpu.VMEM((2, extent * FIRST, channels), bf16),
            pltpu.VMEM((chunks, 2, BLOCK * SECOND, channels), bf16),
            pltpu.VMEM((chunks, 2, BLOCK * SECOND, channels), bf16),
            pltpu.SemaphoreType.DMA((1 + chunks, 2)),
            pltpu.SemaphoreType.DMA((1 + chunks, 2)),
            pltpu.SemaphoreType.DMA((2, 2)),
            pltpu.SemaphoreType.DMA((2, 2)),
            pltpu.SemaphoreType.DMA((chunks,)),
            pltpu.SemaphoreType.DMA((chunks,)),
        ],
        compiler_params=pltpu.CompilerParams(
            collective_id=0, has_side_effects=True, vmem_limit_bytes=40 * 1024 * 1024
        ),
        cost_estimate=pl.CostEstimate(
            flops=2 * cells * channels * channels * 30,
            bytes_accessed=cells * channels * 6,
            transcendentals=0,
        ),
    )(
        features,
        kernel_first.reshape(9 * channels, channels),
        bias_first.reshape(1, channels),
        mixer_first,
        shift_first.reshape(1, channels),
        kernel_second.reshape(9 * channels, channels),
        bias_second.reshape(1, channels),
        mixer_second,
        shift_second.reshape(1, channels),
    )


def solution(mesh):
    return jax.shard_map(
        body,
        mesh=mesh,
        in_specs=(P(("groups", "row"), "col", None), P(), P(), P(), P(), P(), P(), P(), P()),
        out_specs=P(("groups", "row"), "col", None),
        check_vma=False,
    )
```

```python
import functools

import jax
import jax.numpy as jnp
from jax import lax
from jax.experimental import pallas as pl
from jax.experimental.pallas import tpu as pltpu
from jax.sharding import PartitionSpec as P

MESH = pl.DeviceIdType.MESH
FIRST, SECOND = 2, 4
BLOCK = 16


def pack(edge, at, width):
    per = 8 // width
    rows, _, channels = edge.shape
    parts = edge.reshape(rows // per, per, 8, channels)
    lane = lax.broadcasted_iota(jnp.int32, (rows // per, 8, channels), 1)
    packed = None
    for m in range(per):
        shift = (m * width - at) % 8
        part = parts[:, m]
        part = pltpu.roll(part, shift, 1) if shift else part
        packed = part if m == 0 else jnp.where(lane >= m * width, part, packed)
    return packed.reshape(rows * width, channels).astype(jnp.bfloat16)


def unpack(packed, at, width):
    per = 8 // width
    tiles = packed.shape[0] // 8
    channels = packed.shape[1]
    packed = packed.astype(jnp.float32).reshape(tiles, 8, channels)
    parts = []
    for m in range(per):
        shift = (at - m * width) % 8
        parts.append(pltpu.roll(packed, shift, 1) if shift else packed)
    return jnp.stack(parts, axis=1).reshape(tiles * per, 8, channels)


def patch(shifted, spread, lo, rows, left, right):
    extent = shifted.shape[2]
    channels = shifted.shape[3]
    lane = lax.broadcasted_iota(jnp.int32, (rows, 16, channels), 1)
    at = pl.ds(spread + lo, rows)
    strip = unpack(left, 0, spread)
    old = shifted[0, at, 0:16, :].astype(jnp.float32)
    new = jnp.where(lane < spread, jnp.concatenate([strip, strip], axis=1), old)
    shifted[0, at, 0:16, :] = new.astype(jnp.bfloat16)
    strip = unpack(right, 8 - spread, spread)
    old = shifted[2, at, extent - 16 : extent, :].astype(jnp.float32)
    new = jnp.where(lane >= 16 - spread, jnp.concatenate([strip, strip], axis=1), old)
    shifted[2, at, extent - 16 : extent, :] = new.astype(jnp.bfloat16)


def kernel(
    x_in, k1_in, b1_in, m1_in, s1_in, k2_in, b2_in, m2_in, s2_in, out_hbm,
    x, k1, b1, m1, s1, k2, b2, m2, s2,
    xs1, xs2, h, mir, flip, w2, so1, si1, so2, si2, relay, out,
    load, strip_send, strip_recv, rows_send, rows_recv, mir_send, mir_recv,
    relay_send, relay_recv, pass_send, out_sem,
):
    held = (x, k1, b1, m1, s1, k2, b2, m2, s2)
    given = (x_in, k1_in, b1_in, m1_in, s1_in, k2_in, b2_in, m2_in, s2_in)
    loads = [pltpu.make_async_copy(a, b, load.at[n]) for n, (a, b) in enumerate(zip(given, held))]
    for copy in loads:
        copy.start()
    extent, _, channels = x.shape
    chunks = extent // BLOCK
    order = [0] + [chunks - 1] * (chunks > 1) + list(range(1, chunks - 1))
    r, c = lax.axis_index("row"), lax.axis_index("col")
    nr, nc = lax.axis_size("row"), lax.axis_size("col")
    has_up, has_down, has_left, has_right = r > 0, r < nr - 1, c > 0, c < nc - 1
    up, down = {"row": r - 1}, {"row": r + 1}
    left, right = {"col": c - 1}, {"col": c + 1}
    mirror = {"row": c, "col": r}
    off = r != c

    barrier = pltpu.get_barrier_semaphore()
    peers = ((has_up, up), (has_down, down), (has_left, left), (has_right, right), (off, mirror))
    for has, peer in peers:
        @pl.when(has)
        def _():
            pl.semaphore_signal(barrier, inc=1, device_id=peer, device_id_type=MESH)
    count = sum(has.astype(jnp.int32) for has, _ in peers)

    on_diagonal = jnp.logical_not(off)

    @pl.when(off)
    def _():
        pl.semaphore_signal(barrier, inc=1, device_id={"row": c}, device_id_type=MESH)
        pl.semaphore_signal(barrier, inc=1, device_id={"col": r}, device_id_type=MESH)

    def others(work):
        @pl.loop(0, nr)
        def _(other):
            @pl.when(on_diagonal & (other != r))
            def _():
                work(other)

    def greet(other):
        pl.semaphore_signal(barrier, inc=1, device_id={"row": other}, device_id_type=MESH)
        pl.semaphore_signal(barrier, inc=1, device_id={"col": other}, device_id_type=MESH)

    others(greet)
    count = count + jnp.where(off, 2, 2 * (nr - 1))
    loads[0].wait()

    so1[0] = pack(x[:, 0:16, :].astype(jnp.float32)[:, 0:8], 0, FIRST)
    so1[1] = pack(x[:, extent - 16 : extent, :].astype(jnp.float32)[:, 8:16], 8 - FIRST, FIRST)
    pl.semaphore_wait(barrier, count)

    def strips(src, dst, n):
        return (
            (has_left, pltpu.make_async_remote_copy(
                src.at[0], dst.at[1], strip_send.at[n, 0], strip_recv.at[n, 1],
                device_id=left, device_id_type=MESH)),
            (has_right, pltpu.make_async_remote_copy(
                src.at[1], dst.at[0], strip_send.at[n, 1], strip_recv.at[n, 0],
                device_id=right, device_id_type=MESH)),
        )

    def start(copies):
        for has, copy in copies:
            @pl.when(has)
            def _():
                copy.start()

    def finish_strips(copies, dst):
        (hl, to_left), (hr, to_right) = copies

        @pl.when(hl)
        def _():
            to_left.wait_send()
            to_right.wait_recv()

        @pl.when(hr)
        def _():
            to_right.wait_send()
            to_left.wait_recv()

        @pl.when(jnp.logical_not(hl))
        def _():
            dst[0] = jnp.zeros(dst.shape[1:], dst.dtype)

        @pl.when(jnp.logical_not(hr))
        def _():
            dst[1] = jnp.zeros(dst.shape[1:], dst.dtype)

    def halo_rows(shifted, spread, n):
        return (
            (has_up, pltpu.make_async_remote_copy(
                shifted.at[:, spread : 2 * spread], shifted.at[:, extent + spread : extent + 2 * spread],
                rows_send.at[n, 0], rows_recv.at[n, 1], device_id=up, device_id_type=MESH)),
            (has_down, pltpu.make_async_remote_copy(
                shifted.at[:, extent : extent + spread], shifted.at[:, 0:spread],
                rows_send.at[n, 1], rows_recv.at[n, 0], device_id=down, device_id_type=MESH)),
        )

    def finish_rows(copies, shifted, spread):
        (hu, to_up), (hd, to_down) = copies
        zeros = jnp.zeros((3, spread) + shifted.shape[2:], shifted.dtype)

        @pl.when(hu)
        def _():
            to_up.wait_send()
            to_down.wait_recv()

        @pl.when(hd)
        def _():
            to_down.wait_send()
            to_up.wait_recv()

        @pl.when(jnp.logical_not(hu))
        def _():
            shifted[:, 0:spread] = zeros

        @pl.when(jnp.logical_not(hd))
        def _():
            shifted[:, extent + spread : extent + 2 * spread] = zeros

    def spread_rows(shifted, spread, at, cells):
        shifted[1, at] = cells.astype(jnp.bfloat16)
        shifted[0, at] = pltpu.roll(cells, spread, 1).astype(jnp.bfloat16)
        shifted[2, at] = pltpu.roll(cells, extent - spread, 1).astype(jnp.bfloat16)

    first_strips = strips(so1, si1, 0)
    start(first_strips)

    @pl.loop(0, extent // 4)
    def _(step):
        spread_rows(xs1, FIRST, pl.ds(FIRST + step * 4, 4), x[pl.ds(step * 4, 4)].astype(jnp.float32))

    finish_strips(first_strips, si1)

    for k in range(chunks):
        n = BLOCK * FIRST
        patch(xs1, FIRST, k * BLOCK, BLOCK, si1[0, k * n : (k + 1) * n], si1[1, k * n : (k + 1) * n])

    first_rows = halo_rows(xs1, FIRST, 0)
    start(first_rows)
    for copy in loads[1:]:
        copy.wait()
    for p in range(3):
        for q in range(3):
            at = pl.ds((p * 3 + q) * channels, channels)
            w2[at, 0:channels] = k2[at, :]
            w2[at, channels : 2 * channels] = k2[pl.ds((q * 3 + p) * channels, channels), :]
    finish_rows(first_rows, xs1, FIRST)

    half = extent // 2

    def mirror_copy(k):
        cut = pl.ds(k * BLOCK, BLOCK)
        return pltpu.make_async_remote_copy(
            h.at[0:half, cut], mir.at[0:half, cut], mir_send.at[k], mir_recv.at[0, k],
            device_id=mirror, device_id_type=MESH)

    def relay_copy(k, source):
        cut = pl.ds(k * BLOCK, BLOCK)
        return pltpu.make_async_remote_copy(
            h.at[half:extent, cut], relay.at[source, k], relay_send.at[k], relay_recv.at[source, k],
            device_id={"row": c}, device_id_type=MESH)

    def pass_copy(k, source):
        cut = pl.ds(k * BLOCK, BLOCK)
        return pltpu.make_async_remote_copy(
            relay.at[source, k], mir.at[half:extent, cut], pass_send.at[source, k], mir_recv.at[1, k],
            device_id={"col": source}, device_id_type=MESH)

    def pass_chunk(k):
        def work(source):
            relay_copy(k, source).wait_recv()
            pass_copy(k, source).start()

        others(work)

    def local_copy(k):
        cut = pl.ds(k * BLOCK, BLOCK)
        return pltpu.make_async_copy(h.at[:, cut], mir.at[:, cut], mir_send.at[k])

    for n, k in enumerate(order):
        cut = slice(k * BLOCK, (k + 1) * BLOCK)

        @pl.loop(0, extent // BLOCK)
        def _(step):
            row = step * BLOCK
            taps = [
                xs1[q, pl.ds(row + p * FIRST, BLOCK), cut, :].reshape(BLOCK * BLOCK, channels)
                for p in range(3)
                for q in range(3)
            ]
            total = jnp.dot(jnp.concatenate(taps, axis=1), k1[...], preferred_element_type=jnp.float32)
            acted = jnp.maximum(total + b1[...], 0.0).astype(jnp.bfloat16)
            mixed = jnp.dot(acted, m1[...], preferred_element_type=jnp.float32) + s1[...]
            summed = (taps[4].astype(jnp.float32) + mixed).astype(jnp.bfloat16)
            h[pl.ds(row, BLOCK), cut, :] = summed.reshape(BLOCK, BLOCK, channels)

        @pl.when(off)
        def _():
            mirror_copy(k).start()
            relay_copy(k, r).start()

        @pl.when(on_diagonal)
        def _():
            local_copy(k).start()

        if n:
            pass_chunk(order[n - 1])
    pass_chunk(order[-1])

    group = 4

    def out_copy(step):
        at = pl.ds(step * group, group)
        return pltpu.make_async_copy(out.at[at], out_hbm.at[at], out_sem.at[step])

    def second(step):
        row = step * group
        taps = [
            xs2[q, pl.ds(row + p * SECOND, group)].reshape(group * extent, channels)
            for p in range(3)
            for q in range(3)
        ]
        total = jnp.dot(jnp.concatenate(taps, axis=1), w2[...], preferred_element_type=jnp.float32)
        center = taps[4].astype(jnp.float32)
        halves = []
        for side in range(2):
            part = total[:, side * channels : (side + 1) * channels]
            acted = jnp.maximum(part + b2[...], 0.0).astype(jnp.bfloat16)
            mixed = jnp.dot(acted, m2[...], preferred_element_type=jnp.float32) + s2[...]
            halves.append((center + mixed).astype(jnp.bfloat16).astype(jnp.float32))
        mean = jnp.maximum((halves[0] + halves[1]) * 0.5, 0.0)
        out[pl.ds(row, group)] = mean.reshape(group, extent, channels)
        out_copy(step).start()

    def second_range(steps):
        steps = sorted(steps)
        while steps:
            n = 1
            while n < len(steps) and steps[n] == steps[0] + n:
                n += 1
            pl.loop(steps[0], steps[0] + n)(second)
            steps = steps[n:]

    def needs(step):
        lo, hi = step * group - SECOND, step * group + group + SECOND - 1
        return {-1 if at < 0 or at >= extent else at // BLOCK for at in (lo, hi)}

    waiting = set(range(extent // group))
    ready = set()
    done = set()

    second_rows = halo_rows(xs2, SECOND, 1)

    def finish_chunk(k):
        copies = strips(so2.at[k], si2.at[k], 1 + k)
        finish_strips(copies, si2.at[k])
        patch(xs2, SECOND, k * BLOCK, BLOCK, si2[k, 0], si2[k, 1])
        if k == 0:
            start(second_rows[:1])
        if k == chunks - 1:
            start(second_rows[1:])

    for n, k in enumerate(order):
        cut = slice(k * BLOCK, (k + 1) * BLOCK)

        @pl.when(off)
        def _():
            mirror_copy(k).wait()
            relay_copy(k, r).wait_send()
            pass_copy(k, r).wait_recv()

        @pl.when(on_diagonal)
        def _():
            local_copy(k).wait()

        flip[...] = mir[:, cut, :].astype(jnp.float32).reshape(extent * BLOCK, channels)
        for b in range(BLOCK):
            other = flip[pl.ds(b, extent, stride=BLOCK), :]
            row = k * BLOCK + b
            mean = jnp.maximum((h[row].astype(jnp.float32) + other) * 0.5, 0.0)
            spread_rows(xs2, SECOND, pl.ds(SECOND + row, 1), mean.reshape(1, extent, channels))
        at = pl.ds(SECOND + k * BLOCK, BLOCK)
        so2[k, 0] = pack(xs2[1, at, 0:16, :].astype(jnp.float32)[:, 0:8], 0, SECOND)
        so2[k, 1] = pack(
            xs2[1, at, extent - 16 : extent, :].astype(jnp.float32)[:, 8:16], 8 - SECOND, SECOND)
        start(strips(so2.at[k], si2.at[k], 1 + k))
        second_range(ready)
        finish_chunk(k)
        done.add(k)
        if n == min(1, chunks - 1):
            finish_rows(second_rows, xs2, SECOND)
            done.add(-1)
        ready = {step for step in waiting if needs(step) <= done}
        waiting -= ready
        kept = set(sorted(ready)[-3:]) if n == chunks - 2 else set()
        second_range(ready - kept)
        ready = kept

    def drain(source):
        for k in range(chunks):
            pass_copy(k, source).wait_send()

    others(drain)

    @pl.loop(0, extent // group)
    def _(step):
        out_copy(step).wait()


def body(
    features,
    kernel_first,
    bias_first,
    mixer_first,
    shift_first,
    kernel_second,
    bias_second,
    mixer_second,
    shift_second,
):
    extent, _, channels = features.shape
    chunks = extent // BLOCK
    side = lax.axis_size("row")
    bf16 = jnp.bfloat16
    cells = extent * extent
    return pl.pallas_call(
        kernel,
        out_shape=jax.ShapeDtypeStruct(features.shape, jnp.float32),
        in_specs=[pl.BlockSpec(memory_space=pltpu.HBM)] * 9,
        out_specs=pl.BlockSpec(memory_space=pltpu.HBM),
        scratch_shapes=[
            pltpu.VMEM((extent, extent, channels), bf16),
            pltpu.VMEM((9 * channels, channels), bf16),
            pltpu.VMEM((1, channels), jnp.float32),
            pltpu.VMEM((channels, channels), bf16),
            pltpu.VMEM((1, channels), jnp.float32),
            pltpu.VMEM((9 * channels, channels), bf16),
            pltpu.VMEM((1, channels), jnp.float32),
            pltpu.VMEM((channels, channels), bf16),
            pltpu.VMEM((1, channels), jnp.float32),
            pltpu.VMEM((3, extent + 2 * FIRST, extent, channels), bf16),
            pltpu.VMEM((3, extent + 2 * SECOND, extent, channels), bf16),
            pltpu.VMEM((extent, extent, channels), bf16),
            pltpu.VMEM((extent, extent, channels), bf16),
            pltpu.VMEM((extent * BLOCK, channels), jnp.float32),
            pltpu.VMEM((9 * channels, 2 * channels), bf16),
            pltpu.VMEM((2, extent * FIRST, channels), bf16),
            pltpu.VMEM((2, extent * FIRST, channels), bf16),
            pltpu.VMEM((chunks, 2, BLOCK * SECOND, channels), bf16),
            pltpu.VMEM((chunks, 2, BLOCK * SECOND, channels), bf16),
            pltpu.VMEM((side, chunks, extent // 2, BLOCK, channels), bf16),
            pltpu.VMEM((extent, extent, channels), jnp.float32),
            pltpu.SemaphoreType.DMA((9,)),
            pltpu.SemaphoreType.DMA((1 + chunks, 2)),
            pltpu.SemaphoreType.DMA((1 + chunks, 2)),
            pltpu.SemaphoreType.DMA((2, 2)),
            pltpu.SemaphoreType.DMA((2, 2)),
            pltpu.SemaphoreType.DMA((chunks,)),
            pltpu.SemaphoreType.DMA((2, chunks)),
            pltpu.SemaphoreType.DMA((chunks,)),
            pltpu.SemaphoreType.DMA((side, chunks)),
            pltpu.SemaphoreType.DMA((side, chunks)),
            pltpu.SemaphoreType.DMA((extent // 4,)),
        ],
        compiler_params=pltpu.CompilerParams(
            collective_id=0, has_side_effects=True, vmem_limit_bytes=60 * 1024 * 1024
        ),
        cost_estimate=pl.CostEstimate(
            flops=2 * cells * channels * channels * 30,
            bytes_accessed=cells * channels * 6,
            transcendentals=0,
        ),
    )(
        features,
        kernel_first.reshape(9 * channels, channels),
        bias_first.reshape(1, channels),
        mixer_first,
        shift_first.reshape(1, channels),
        kernel_second.reshape(9 * channels, channels),
        bias_second.reshape(1, channels),
        mixer_second,
        shift_second.reshape(1, channels),
    )


def solution(mesh):
    return jax.shard_map(
        body,
        mesh=mesh,
        in_specs=(P(("groups", "row"), "col", None), P(), P(), P(), P(), P(), P(), P(), P()),
        out_specs=P(("groups", "row"), "col", None),
        check_vma=False,
    )
```

```python
import functools

import jax
import jax.numpy as jnp
from jax import lax
from jax.experimental import pallas as pl
from jax.experimental.pallas import tpu as pltpu
from jax.sharding import PartitionSpec as P

MESH = pl.DeviceIdType.MESH
FIRST, SECOND = 2, 4
BLOCK = 16


def pack(edge, at, width):
    per = 8 // width
    rows, _, channels = edge.shape
    parts = edge.reshape(rows // per, per, 8, channels)
    lane = lax.broadcasted_iota(jnp.int32, (rows // per, 8, channels), 1)
    packed = None
    for m in range(per):
        shift = (m * width - at) % 8
        part = parts[:, m]
        part = pltpu.roll(part, shift, 1) if shift else part
        packed = part if m == 0 else jnp.where(lane >= m * width, part, packed)
    return packed.reshape(rows * width, channels).astype(jnp.bfloat16)


def unpack(packed, at, width):
    per = 8 // width
    tiles = packed.shape[0] // 8
    channels = packed.shape[1]
    packed = packed.astype(jnp.float32).reshape(tiles, 8, channels)
    parts = []
    for m in range(per):
        shift = (at - m * width) % 8
        parts.append(pltpu.roll(packed, shift, 1) if shift else packed)
    return jnp.stack(parts, axis=1).reshape(tiles * per, 8, channels)


def patch(shifted, spread, lo, rows, left, right):
    extent = shifted.shape[2]
    channels = shifted.shape[3]
    lane = lax.broadcasted_iota(jnp.int32, (rows, 16, channels), 1)
    at = pl.ds(spread + lo, rows)
    strip = unpack(left, 0, spread)
    old = shifted[0, at, 0:16, :].astype(jnp.float32)
    new = jnp.where(lane < spread, jnp.concatenate([strip, strip], axis=1), old)
    shifted[0, at, 0:16, :] = new.astype(jnp.bfloat16)
    strip = unpack(right, 8 - spread, spread)
    old = shifted[2, at, extent - 16 : extent, :].astype(jnp.float32)
    new = jnp.where(lane >= 16 - spread, jnp.concatenate([strip, strip], axis=1), old)
    shifted[2, at, extent - 16 : extent, :] = new.astype(jnp.bfloat16)


def kernel(
    x_in, k1_in, b1_in, m1_in, s1_in, k2_in, b2_in, m2_in, s2_in, out_hbm,
    x, k1, b1, m1, s1, k2, b2, m2, s2,
    xs1, xs2, h, mir, flip, w2, so1, si1, so2, si2, relay, out,
    load, strip_send, strip_recv, rows_send, rows_recv, mir_send, mir_recv,
    relay_send, relay_recv, pass_send, out_sem,
):
    held = (x, k1, b1, m1, s1, k2, b2, m2, s2)
    given = (x_in, k1_in, b1_in, m1_in, s1_in, k2_in, b2_in, m2_in, s2_in)
    loads = [pltpu.make_async_copy(a, b, load.at[n]) for n, (a, b) in enumerate(zip(given, held))]
    for copy in loads:
        copy.start()
    extent, _, channels = x.shape
    chunks = extent // BLOCK
    order = [0] + [chunks - 1] * (chunks > 1) + list(range(1, chunks - 1))
    r, c = lax.axis_index("row"), lax.axis_index("col")
    nr, nc = lax.axis_size("row"), lax.axis_size("col")
    has_up, has_down, has_left, has_right = r > 0, r < nr - 1, c > 0, c < nc - 1
    up, down = {"row": r - 1}, {"row": r + 1}
    left, right = {"col": c - 1}, {"col": c + 1}
    mirror = {"row": c, "col": r}
    off = r != c

    barrier = pltpu.get_barrier_semaphore()
    peers = ((has_up, up), (has_down, down), (has_left, left), (has_right, right), (off, mirror))
    for has, peer in peers:
        @pl.when(has)
        def _():
            pl.semaphore_signal(barrier, inc=1, device_id=peer, device_id_type=MESH)
    count = sum(has.astype(jnp.int32) for has, _ in peers)

    on_diagonal = jnp.logical_not(off)

    @pl.when(off)
    def _():
        pl.semaphore_signal(barrier, inc=1, device_id={"row": c}, device_id_type=MESH)
        pl.semaphore_signal(barrier, inc=1, device_id={"col": r}, device_id_type=MESH)

    def others(work):
        @pl.loop(0, nr)
        def _(other):
            @pl.when(on_diagonal & (other != r))
            def _():
                work(other)

    def greet(other):
        pl.semaphore_signal(barrier, inc=1, device_id={"row": other}, device_id_type=MESH)
        pl.semaphore_signal(barrier, inc=1, device_id={"col": other}, device_id_type=MESH)

    others(greet)
    count = count + jnp.where(off, 2, 2 * (nr - 1))
    loads[0].wait()

    so1[0] = pack(x[:, 0:16, :].astype(jnp.float32)[:, 0:8], 0, FIRST)
    so1[1] = pack(x[:, extent - 16 : extent, :].astype(jnp.float32)[:, 8:16], 8 - FIRST, FIRST)
    pl.semaphore_wait(barrier, count)

    def strips(src, dst, n):
        return (
            (has_left, pltpu.make_async_remote_copy(
                src.at[0], dst.at[1], strip_send.at[n, 0], strip_recv.at[n, 1],
                device_id=left, device_id_type=MESH)),
            (has_right, pltpu.make_async_remote_copy(
                src.at[1], dst.at[0], strip_send.at[n, 1], strip_recv.at[n, 0],
                device_id=right, device_id_type=MESH)),
        )

    def start(copies):
        for has, copy in copies:
            @pl.when(has)
            def _():
                copy.start()

    def finish_strips(copies, dst):
        (hl, to_left), (hr, to_right) = copies

        @pl.when(hl)
        def _():
            to_left.wait_send()
            to_right.wait_recv()

        @pl.when(hr)
        def _():
            to_right.wait_send()
            to_left.wait_recv()

        @pl.when(jnp.logical_not(hl))
        def _():
            dst[0] = jnp.zeros(dst.shape[1:], dst.dtype)

        @pl.when(jnp.logical_not(hr))
        def _():
            dst[1] = jnp.zeros(dst.shape[1:], dst.dtype)

    def halo_rows(shifted, spread, n):
        return (
            (has_up, pltpu.make_async_remote_copy(
                shifted.at[:, spread : 2 * spread], shifted.at[:, extent + spread : extent + 2 * spread],
                rows_send.at[n, 0], rows_recv.at[n, 1], device_id=up, device_id_type=MESH)),
            (has_down, pltpu.make_async_remote_copy(
                shifted.at[:, extent : extent + spread], shifted.at[:, 0:spread],
                rows_send.at[n, 1], rows_recv.at[n, 0], device_id=down, device_id_type=MESH)),
        )

    def finish_rows(copies, shifted, spread):
        (hu, to_up), (hd, to_down) = copies
        zeros = jnp.zeros((3, spread) + shifted.shape[2:], shifted.dtype)

        @pl.when(hu)
        def _():
            to_up.wait_send()
            to_down.wait_recv()

        @pl.when(hd)
        def _():
            to_down.wait_send()
            to_up.wait_recv()

        @pl.when(jnp.logical_not(hu))
        def _():
            shifted[:, 0:spread] = zeros

        @pl.when(jnp.logical_not(hd))
        def _():
            shifted[:, extent + spread : extent + 2 * spread] = zeros

    def spread_rows(shifted, spread, at, cells):
        shifted[1, at] = cells.astype(jnp.bfloat16)
        shifted[0, at] = pltpu.roll(cells, spread, 1).astype(jnp.bfloat16)
        shifted[2, at] = pltpu.roll(cells, extent - spread, 1).astype(jnp.bfloat16)

    first_strips = strips(so1, si1, 0)
    start(first_strips)

    @pl.loop(0, extent // 4)
    def _(step):
        spread_rows(xs1, FIRST, pl.ds(FIRST + step * 4, 4), x[pl.ds(step * 4, 4)].astype(jnp.float32))

    finish_strips(first_strips, si1)

    for k in range(chunks):
        n = BLOCK * FIRST
        patch(xs1, FIRST, k * BLOCK, BLOCK, si1[0, k * n : (k + 1) * n], si1[1, k * n : (k + 1) * n])

    first_rows = halo_rows(xs1, FIRST, 0)
    start(first_rows)
    for copy in loads[1:]:
        copy.wait()
    for p in range(3):
        for q in range(3):
            at = pl.ds((p * 3 + q) * channels, channels)
            w2[at, 0:channels] = k2[at, :]
            w2[at, channels : 2 * channels] = k2[pl.ds((q * 3 + p) * channels, channels), :]
    finish_rows(first_rows, xs1, FIRST)

    half = extent // 2

    def mirror_copy(k):
        cut = pl.ds(k * BLOCK, BLOCK)
        return pltpu.make_async_remote_copy(
            h.at[0:half, cut], mir.at[0:half, cut], mir_send.at[k], mir_recv.at[0, k],
            device_id=mirror, device_id_type=MESH)

    def relay_copy(k, source):
        cut = pl.ds(k * BLOCK, BLOCK)
        return pltpu.make_async_remote_copy(
            h.at[half:extent, cut], relay.at[source, k], relay_send.at[k], relay_recv.at[source, k],
            device_id={"row": c}, device_id_type=MESH)

    def pass_copy(k, source):
        cut = pl.ds(k * BLOCK, BLOCK)
        return pltpu.make_async_remote_copy(
            relay.at[source, k], mir.at[half:extent, cut], pass_send.at[source, k], mir_recv.at[1, k],
            device_id={"col": source}, device_id_type=MESH)

    def pass_chunk(k):
        def work(source):
            relay_copy(k, source).wait_recv()
            pass_copy(k, source).start()

        others(work)

    def local_copy(k):
        cut = pl.ds(k * BLOCK, BLOCK)
        return pltpu.make_async_copy(h.at[:, cut], mir.at[:, cut], mir_send.at[k])

    def send_chunk(k):
        @pl.when(off)
        def _():
            mirror_copy(k).start()
            relay_copy(k, r).start()

        @pl.when(on_diagonal)
        def _():
            local_copy(k).start()

    tall = 2 * BLOCK
    for n, k in enumerate(order):
        cut = slice(k * BLOCK, (k + 1) * BLOCK)

        @pl.loop(0, extent // tall)
        def _(step):
            row = step * tall
            taps = [
                xs1[q, pl.ds(row + p * FIRST, tall), cut, :].reshape(tall * BLOCK, channels)
                for p in range(3)
                for q in range(3)
            ]
            total = jnp.dot(jnp.concatenate(taps, axis=1), k1[...], preferred_element_type=jnp.float32)
            acted = jnp.maximum(total + b1[...], 0.0).astype(jnp.bfloat16)
            mixed = jnp.dot(acted, m1[...], preferred_element_type=jnp.float32) + s1[...]
            summed = (taps[4].astype(jnp.float32) + mixed).astype(jnp.bfloat16)
            h[pl.ds(row, tall), cut, :] = summed.reshape(tall, BLOCK, channels)

        if n < chunks - 1:
            send_chunk(k)
        if n:
            pass_chunk(order[n - 1])

    group = 8

    def out_copy(step):
        at = pl.ds(step * group, group)
        return pltpu.make_async_copy(out.at[at], out_hbm.at[at], out_sem.at[step])

    def second(step):
        row = step * group
        taps = [
            xs2[q, pl.ds(row + p * SECOND, group)].reshape(group * extent, channels)
            for p in range(3)
            for q in range(3)
        ]
        total = jnp.dot(jnp.concatenate(taps, axis=1), w2[...], preferred_element_type=jnp.float32)
        center = taps[4].astype(jnp.float32)
        halves = []
        for side in range(2):
            part = total[:, side * channels : (side + 1) * channels]
            acted = jnp.maximum(part + b2[...], 0.0).astype(jnp.bfloat16)
            mixed = jnp.dot(acted, m2[...], preferred_element_type=jnp.float32) + s2[...]
            halves.append((center + mixed).astype(jnp.bfloat16).astype(jnp.float32))
        mean = jnp.maximum((halves[0] + halves[1]) * 0.5, 0.0)
        out[pl.ds(row, group)] = mean.reshape(group, extent, channels)
        out_copy(step).start()

    def second_range(steps):
        steps = sorted(steps)
        while steps:
            n = 1
            while n < len(steps) and steps[n] == steps[0] + n:
                n += 1
            pl.loop(steps[0], steps[0] + n)(second)
            steps = steps[n:]

    def needs(step):
        lo, hi = step * group - SECOND, step * group + group + SECOND - 1
        return {-1 if at < 0 or at >= extent else at // BLOCK for at in (lo, hi)}

    waiting = set(range(extent // group))
    done = set()

    second_rows = halo_rows(xs2, SECOND, 1)

    def finish_chunk(k):
        copies = strips(so2.at[k], si2.at[k], 1 + k)
        finish_strips(copies, si2.at[k])
        patch(xs2, SECOND, k * BLOCK, BLOCK, si2[k, 0], si2[k, 1])
        if k == 0:
            start(second_rows[:1])
        if k == chunks - 1:
            start(second_rows[1:])

    for n, k in enumerate(order):
        cut = slice(k * BLOCK, (k + 1) * BLOCK)

        @pl.when(off)
        def _():
            mirror_copy(k).wait()
            relay_copy(k, r).wait_send()
            pass_copy(k, r).wait_recv()

        @pl.when(on_diagonal)
        def _():
            local_copy(k).wait()

        flip[...] = mir[:, cut, :].astype(jnp.float32).reshape(extent * BLOCK, channels)
        for b in range(BLOCK):
            other = flip[pl.ds(b, extent, stride=BLOCK), :]
            row = k * BLOCK + b
            mean = jnp.maximum((h[row].astype(jnp.float32) + other) * 0.5, 0.0)
            spread_rows(xs2, SECOND, pl.ds(SECOND + row, 1), mean.reshape(1, extent, channels))
        at = pl.ds(SECOND + k * BLOCK, BLOCK)
        so2[k, 0] = pack(xs2[1, at, 0:16, :].astype(jnp.float32)[:, 0:8], 0, SECOND)
        so2[k, 1] = pack(
            xs2[1, at, extent - 16 : extent, :].astype(jnp.float32)[:, 8:16], 8 - SECOND, SECOND)
        start(strips(so2.at[k], si2.at[k], 1 + k))
        if n == chunks - 2:
            send_chunk(order[-1])
            pass_chunk(order[-1])
            for other in order[:-1]:
                finish_chunk(other)
            finish_rows(second_rows, xs2, SECOND)
            done |= {-1, *order[:-1]}
            ready = {step for step in waiting if needs(step) <= done}
            waiting -= ready
            kept = set(sorted(ready)[-2:])
            second_range(ready - kept)
    second_range(kept)
    finish_chunk(order[-1])
    second_range(waiting)

    def drain(source):
        for k in range(chunks):
            pass_copy(k, source).wait_send()

    others(drain)

    @pl.loop(0, extent // group)
    def _(step):
        out_copy(step).wait()


def body(
    features,
    kernel_first,
    bias_first,
    mixer_first,
    shift_first,
    kernel_second,
    bias_second,
    mixer_second,
    shift_second,
):
    extent, _, channels = features.shape
    chunks = extent // BLOCK
    side = lax.axis_size("row")
    bf16 = jnp.bfloat16
    cells = extent * extent
    return pl.pallas_call(
        kernel,
        out_shape=jax.ShapeDtypeStruct(features.shape, jnp.float32),
        in_specs=[pl.BlockSpec(memory_space=pltpu.HBM)] * 9,
        out_specs=pl.BlockSpec(memory_space=pltpu.HBM),
        scratch_shapes=[
            pltpu.VMEM((extent, extent, channels), bf16),
            pltpu.VMEM((9 * channels, channels), bf16),
            pltpu.VMEM((1, channels), jnp.float32),
            pltpu.VMEM((channels, channels), bf16),
            pltpu.VMEM((1, channels), jnp.float32),
            pltpu.VMEM((9 * channels, channels), bf16),
            pltpu.VMEM((1, channels), jnp.float32),
            pltpu.VMEM((channels, channels), bf16),
            pltpu.VMEM((1, channels), jnp.float32),
            pltpu.VMEM((3, extent + 2 * FIRST, extent, channels), bf16),
            pltpu.VMEM((3, extent + 2 * SECOND, extent, channels), bf16),
            pltpu.VMEM((extent, extent, channels), bf16),
            pltpu.VMEM((extent, extent, channels), bf16),
            pltpu.VMEM((extent * BLOCK, channels), jnp.float32),
            pltpu.VMEM((9 * channels, 2 * channels), bf16),
            pltpu.VMEM((2, extent * FIRST, channels), bf16),
            pltpu.VMEM((2, extent * FIRST, channels), bf16),
            pltpu.VMEM((chunks, 2, BLOCK * SECOND, channels), bf16),
            pltpu.VMEM((chunks, 2, BLOCK * SECOND, channels), bf16),
            pltpu.VMEM((side, chunks, extent // 2, BLOCK, channels), bf16),
            pltpu.VMEM((extent, extent, channels), jnp.float32),
            pltpu.SemaphoreType.DMA((9,)),
            pltpu.SemaphoreType.DMA((1 + chunks, 2)),
            pltpu.SemaphoreType.DMA((1 + chunks, 2)),
            pltpu.SemaphoreType.DMA((2, 2)),
            pltpu.SemaphoreType.DMA((2, 2)),
            pltpu.SemaphoreType.DMA((chunks,)),
            pltpu.SemaphoreType.DMA((2, chunks)),
            pltpu.SemaphoreType.DMA((chunks,)),
            pltpu.SemaphoreType.DMA((side, chunks)),
            pltpu.SemaphoreType.DMA((side, chunks)),
            pltpu.SemaphoreType.DMA((extent // 8,)),
        ],
        compiler_params=pltpu.CompilerParams(
            collective_id=0, has_side_effects=True, vmem_limit_bytes=60 * 1024 * 1024
        ),
        cost_estimate=pl.CostEstimate(
            flops=2 * cells * channels * channels * 30,
            bytes_accessed=cells * channels * 6,
            transcendentals=0,
        ),
    )(
        features,
        kernel_first.reshape(9 * channels, channels),
        bias_first.reshape(1, channels),
        mixer_first,
        shift_first.reshape(1, channels),
        kernel_second.reshape(9 * channels, channels),
        bias_second.reshape(1, channels),
        mixer_second,
        shift_second.reshape(1, channels),
    )


def solution(mesh):
    return jax.shard_map(
        body,
        mesh=mesh,
        in_specs=(P(("groups", "row"), "col", None), P(), P(), P(), P(), P(), P(), P(), P()),
        out_specs=P(("groups", "row"), "col", None),
        check_vma=False,
    )
```

```python
import functools

import jax
import jax.numpy as jnp
from jax import lax
from jax.experimental import pallas as pl
from jax.experimental.pallas import tpu as pltpu
from jax.sharding import PartitionSpec as P

MESH = pl.DeviceIdType.MESH
FIRST, SECOND = 2, 4
BLOCK = 16


def pack(edge, at, width):
    per = 8 // width
    rows, _, channels = edge.shape
    parts = edge.reshape(rows // per, per, 8, channels)
    lane = lax.broadcasted_iota(jnp.int32, (rows // per, 8, channels), 1)
    packed = None
    for m in range(per):
        shift = (m * width - at) % 8
        part = parts[:, m]
        part = pltpu.roll(part, shift, 1) if shift else part
        packed = part if m == 0 else jnp.where(lane >= m * width, part, packed)
    return packed.reshape(rows * width, channels).astype(jnp.bfloat16)


def unpack(packed, at, width):
    per = 8 // width
    tiles = packed.shape[0] // 8
    channels = packed.shape[1]
    packed = packed.astype(jnp.float32).reshape(tiles, 8, channels)
    parts = []
    for m in range(per):
        shift = (at - m * width) % 8
        parts.append(pltpu.roll(packed, shift, 1) if shift else packed)
    return jnp.stack(parts, axis=1).reshape(tiles * per, 8, channels)


def patch(shifted, spread, lo, rows, left, right):
    extent = shifted.shape[2]
    channels = shifted.shape[3]
    lane = lax.broadcasted_iota(jnp.int32, (rows, 16, channels), 1)
    at = pl.ds(spread + lo, rows)
    strip = unpack(left, 0, spread)
    old = shifted[0, at, 0:16, :].astype(jnp.float32)
    new = jnp.where(lane < spread, jnp.concatenate([strip, strip], axis=1), old)
    shifted[0, at, 0:16, :] = new.astype(jnp.bfloat16)
    strip = unpack(right, 8 - spread, spread)
    old = shifted[2, at, extent - 16 : extent, :].astype(jnp.float32)
    new = jnp.where(lane >= 16 - spread, jnp.concatenate([strip, strip], axis=1), old)
    shifted[2, at, extent - 16 : extent, :] = new.astype(jnp.bfloat16)


def kernel(
    x_in, k1_in, b1_in, m1_in, s1_in, k2_in, b2_in, m2_in, s2_in, out_hbm,
    x, k1, b1, m1, s1, k2, b2, m2, s2,
    xs1, xs2, h, mir, flip, w2, so1, si1, so2, si2, relay, out,
    load, strip_send, strip_recv, rows_send, rows_recv, mir_send, mir_recv,
    relay_send, relay_recv, pass_send, out_sem,
):
    held = (x, k1, b1, m1, s1, k2, b2, m2, s2)
    given = (x_in, k1_in, b1_in, m1_in, s1_in, k2_in, b2_in, m2_in, s2_in)
    loads = [pltpu.make_async_copy(a, b, load.at[n]) for n, (a, b) in enumerate(zip(given, held))]
    for copy in loads:
        copy.start()
    extent, _, channels = x.shape
    chunks = extent // BLOCK
    order = [0] + [chunks - 1] * (chunks > 1) + list(range(1, chunks - 1))
    r, c = lax.axis_index("row"), lax.axis_index("col")
    nr, nc = lax.axis_size("row"), lax.axis_size("col")
    has_up, has_down, has_left, has_right = r > 0, r < nr - 1, c > 0, c < nc - 1
    up, down = {"row": r - 1}, {"row": r + 1}
    left, right = {"col": c - 1}, {"col": c + 1}
    mirror = {"row": c, "col": r}
    off = r != c

    barrier = pltpu.get_barrier_semaphore()
    peers = ((has_up, up), (has_down, down), (has_left, left), (has_right, right), (off, mirror))
    for has, peer in peers:
        @pl.when(has)
        def _():
            pl.semaphore_signal(barrier, inc=1, device_id=peer, device_id_type=MESH)
    count = sum(has.astype(jnp.int32) for has, _ in peers)

    on_diagonal = jnp.logical_not(off)

    @pl.when(off)
    def _():
        pl.semaphore_signal(barrier, inc=1, device_id={"row": c}, device_id_type=MESH)
        pl.semaphore_signal(barrier, inc=1, device_id={"col": r}, device_id_type=MESH)

    def others(work):
        @pl.loop(0, nr)
        def _(other):
            @pl.when(on_diagonal & (other != r))
            def _():
                work(other)

    def greet(other):
        pl.semaphore_signal(barrier, inc=1, device_id={"row": other}, device_id_type=MESH)
        pl.semaphore_signal(barrier, inc=1, device_id={"col": other}, device_id_type=MESH)

    others(greet)
    count = count + jnp.where(off, 2, 2 * (nr - 1))
    loads[0].wait()

    so1[0] = pack(x[:, 0:16, :].astype(jnp.float32)[:, 0:8], 0, FIRST)
    so1[1] = pack(x[:, extent - 16 : extent, :].astype(jnp.float32)[:, 8:16], 8 - FIRST, FIRST)
    pl.semaphore_wait(barrier, count)

    def strips(src, dst, n):
        return (
            (has_left, pltpu.make_async_remote_copy(
                src.at[0], dst.at[1], strip_send.at[n, 0], strip_recv.at[n, 1],
                device_id=left, device_id_type=MESH)),
            (has_right, pltpu.make_async_remote_copy(
                src.at[1], dst.at[0], strip_send.at[n, 1], strip_recv.at[n, 0],
                device_id=right, device_id_type=MESH)),
        )

    def start(copies):
        for has, copy in copies:
            @pl.when(has)
            def _():
                copy.start()

    def finish_strips(copies, dst):
        (hl, to_left), (hr, to_right) = copies

        @pl.when(hl)
        def _():
            to_left.wait_send()
            to_right.wait_recv()

        @pl.when(hr)
        def _():
            to_right.wait_send()
            to_left.wait_recv()

        @pl.when(jnp.logical_not(hl))
        def _():
            dst[0] = jnp.zeros(dst.shape[1:], dst.dtype)

        @pl.when(jnp.logical_not(hr))
        def _():
            dst[1] = jnp.zeros(dst.shape[1:], dst.dtype)

    def halo_rows(shifted, spread, n):
        return (
            (has_up, pltpu.make_async_remote_copy(
                shifted.at[:, spread : 2 * spread], shifted.at[:, extent + spread : extent + 2 * spread],
                rows_send.at[n, 0], rows_recv.at[n, 1], device_id=up, device_id_type=MESH)),
            (has_down, pltpu.make_async_remote_copy(
                shifted.at[:, extent : extent + spread], shifted.at[:, 0:spread],
                rows_send.at[n, 1], rows_recv.at[n, 0], device_id=down, device_id_type=MESH)),
        )

    def finish_rows(copies, shifted, spread):
        (hu, to_up), (hd, to_down) = copies
        zeros = jnp.zeros((3, spread) + shifted.shape[2:], shifted.dtype)

        @pl.when(hu)
        def _():
            to_up.wait_send()
            to_down.wait_recv()

        @pl.when(hd)
        def _():
            to_down.wait_send()
            to_up.wait_recv()

        @pl.when(jnp.logical_not(hu))
        def _():
            shifted[:, 0:spread] = zeros

        @pl.when(jnp.logical_not(hd))
        def _():
            shifted[:, extent + spread : extent + 2 * spread] = zeros

    def spread_rows(shifted, spread, at, cells):
        shifted[1, at] = cells.astype(jnp.bfloat16)
        shifted[0, at] = pltpu.roll(cells, spread, 1).astype(jnp.bfloat16)
        shifted[2, at] = pltpu.roll(cells, extent - spread, 1).astype(jnp.bfloat16)

    first_strips = strips(so1, si1, 0)
    start(first_strips)

    @pl.loop(0, extent // 4)
    def _(step):
        spread_rows(xs1, FIRST, pl.ds(FIRST + step * 4, 4), x[pl.ds(step * 4, 4)].astype(jnp.float32))

    finish_strips(first_strips, si1)

    for k in range(chunks):
        n = BLOCK * FIRST
        patch(xs1, FIRST, k * BLOCK, BLOCK, si1[0, k * n : (k + 1) * n], si1[1, k * n : (k + 1) * n])

    first_rows = halo_rows(xs1, FIRST, 0)
    start(first_rows)
    for copy in loads[1:]:
        copy.wait()
    for p in range(3):
        for q in range(3):
            at = pl.ds((p * 3 + q) * channels, channels)
            w2[at, 0:channels] = k2[at, :]
            w2[at, channels : 2 * channels] = k2[pl.ds((q * 3 + p) * channels, channels), :]

    def sums(row, tall, cut):
        taps = [
            xs1[q, pl.ds(row + p * FIRST, tall), cut, :].reshape(tall * BLOCK, channels)
            for p in range(3)
            for q in range(3)
        ]
        total = jnp.dot(jnp.concatenate(taps, axis=1), k1[...], preferred_element_type=jnp.float32)
        acted = jnp.maximum(total + b1[...], 0.0).astype(jnp.bfloat16)
        mixed = jnp.dot(acted, m1[...], preferred_element_type=jnp.float32) + s1[...]
        summed = (taps[4].astype(jnp.float32) + mixed).astype(jnp.bfloat16)
        h[pl.ds(row, tall), cut, :] = summed.reshape(tall, BLOCK, channels)

    @pl.loop(0, extent // BLOCK - 2, step=2)
    def _(step):
        sums((step + 1) * BLOCK, 2 * BLOCK, slice(0, BLOCK))

    finish_rows(first_rows, xs1, FIRST)

    half = extent // 2

    def mirror_copy(k):
        cut = pl.ds(k * BLOCK, BLOCK)
        return pltpu.make_async_remote_copy(
            h.at[0:half, cut], mir.at[0:half, cut], mir_send.at[k], mir_recv.at[0, k],
            device_id=mirror, device_id_type=MESH)

    def relay_copy(k, source):
        cut = pl.ds(k * BLOCK, BLOCK)
        return pltpu.make_async_remote_copy(
            h.at[half:extent, cut], relay.at[source, k], relay_send.at[k], relay_recv.at[source, k],
            device_id={"row": c}, device_id_type=MESH)

    def pass_copy(k, source):
        cut = pl.ds(k * BLOCK, BLOCK)
        return pltpu.make_async_remote_copy(
            relay.at[source, k], mir.at[half:extent, cut], pass_send.at[source, k], mir_recv.at[1, k],
            device_id={"col": source}, device_id_type=MESH)

    def pass_chunk(k):
        def work(source):
            relay_copy(k, source).wait_recv()
            pass_copy(k, source).start()

        others(work)

    def local_copy(k):
        cut = pl.ds(k * BLOCK, BLOCK)
        return pltpu.make_async_copy(h.at[:, cut], mir.at[:, cut], mir_send.at[k])

    def send_chunk(k):
        @pl.when(off)
        def _():
            mirror_copy(k).start()
            relay_copy(k, r).start()

        @pl.when(on_diagonal)
        def _():
            local_copy(k).start()

    for n, k in enumerate(order):
        cut = slice(k * BLOCK, (k + 1) * BLOCK)

        if n:
            @pl.loop(0, extent // (2 * BLOCK))
            def _(step):
                sums(step * 2 * BLOCK, 2 * BLOCK, cut)
        else:
            sums(0, BLOCK, cut)
            sums(extent - BLOCK, BLOCK, cut)

        if n < chunks - 1:
            send_chunk(k)
        if n:
            pass_chunk(order[n - 1])

    group = 8

    def out_copy(step):
        at = pl.ds(step * group, group)
        return pltpu.make_async_copy(out.at[at], out_hbm.at[at], out_sem.at[step])

    def second(step):
        row = step * group
        taps = [
            xs2[q, pl.ds(row + p * SECOND, group)].reshape(group * extent, channels)
            for p in range(3)
            for q in range(3)
        ]
        total = jnp.dot(jnp.concatenate(taps, axis=1), w2[...], preferred_element_type=jnp.float32)
        center = taps[4].astype(jnp.float32)
        halves = []
        for side in range(2):
            part = total[:, side * channels : (side + 1) * channels]
            acted = jnp.maximum(part + b2[...], 0.0).astype(jnp.bfloat16)
            mixed = jnp.dot(acted, m2[...], preferred_element_type=jnp.float32) + s2[...]
            halves.append((center + mixed).astype(jnp.bfloat16).astype(jnp.float32))
        mean = jnp.maximum((halves[0] + halves[1]) * 0.5, 0.0)
        out[pl.ds(row, group)] = mean.reshape(group, extent, channels)
        out_copy(step).start()

    def second_range(steps):
        steps = sorted(steps)
        while steps:
            n = 1
            while n < len(steps) and steps[n] == steps[0] + n:
                n += 1
            pl.loop(steps[0], steps[0] + n)(second)
            steps = steps[n:]

    def needs(step):
        lo, hi = step * group - SECOND, step * group + group + SECOND - 1
        return {-1 if at < 0 or at >= extent else at // BLOCK for at in (lo, hi)}

    waiting = set(range(extent // group))
    done = set()

    second_rows = halo_rows(xs2, SECOND, 1)

    def finish_chunk(k):
        copies = strips(so2.at[k], si2.at[k], 1 + k)
        finish_strips(copies, si2.at[k])
        patch(xs2, SECOND, k * BLOCK, BLOCK, si2[k, 0], si2[k, 1])
        if k == 0:
            start(second_rows[:1])
        if k == chunks - 1:
            start(second_rows[1:])

    for n, k in enumerate(order):
        cut = slice(k * BLOCK, (k + 1) * BLOCK)

        @pl.when(off)
        def _():
            mirror_copy(k).wait()
            relay_copy(k, r).wait_send()
            pass_copy(k, r).wait_recv()

        @pl.when(on_diagonal)
        def _():
            local_copy(k).wait()

        flip[...] = mir[:, cut, :].astype(jnp.float32).reshape(extent * BLOCK, channels)
        for b in range(BLOCK):
            other = flip[pl.ds(b, extent, stride=BLOCK), :]
            row = k * BLOCK + b
            mean = jnp.maximum((h[row].astype(jnp.float32) + other) * 0.5, 0.0)
            spread_rows(xs2, SECOND, pl.ds(SECOND + row, 1), mean.reshape(1, extent, channels))
        at = pl.ds(SECOND + k * BLOCK, BLOCK)
        so2[k, 0] = pack(xs2[1, at, 0:16, :].astype(jnp.float32)[:, 0:8], 0, SECOND)
        so2[k, 1] = pack(
            xs2[1, at, extent - 16 : extent, :].astype(jnp.float32)[:, 8:16], 8 - SECOND, SECOND)
        start(strips(so2.at[k], si2.at[k], 1 + k))
        if n == chunks - 2:
            send_chunk(order[-1])
            pass_chunk(order[-1])
            for other in order[:-1]:
                finish_chunk(other)
            finish_rows(second_rows, xs2, SECOND)
            done |= {-1, *order[:-1]}
            ready = {step for step in waiting if needs(step) <= done}
            waiting -= ready
            kept = set(sorted(ready)[-2:])
            second_range(ready - kept)
    second_range(kept)
    finish_chunk(order[-1])
    second_range(waiting)

    def drain(source):
        for k in range(chunks):
            pass_copy(k, source).wait_send()

    others(drain)

    @pl.loop(0, extent // group)
    def _(step):
        out_copy(step).wait()


def body(
    features,
    kernel_first,
    bias_first,
    mixer_first,
    shift_first,
    kernel_second,
    bias_second,
    mixer_second,
    shift_second,
):
    extent, _, channels = features.shape
    chunks = extent // BLOCK
    side = lax.axis_size("row")
    bf16 = jnp.bfloat16
    cells = extent * extent
    return pl.pallas_call(
        kernel,
        out_shape=jax.ShapeDtypeStruct(features.shape, jnp.float32),
        in_specs=[pl.BlockSpec(memory_space=pltpu.HBM)] * 9,
        out_specs=pl.BlockSpec(memory_space=pltpu.HBM),
        scratch_shapes=[
            pltpu.VMEM((extent, extent, channels), bf16),
            pltpu.VMEM((9 * channels, channels), bf16),
            pltpu.VMEM((1, channels), jnp.float32),
            pltpu.VMEM((channels, channels), bf16),
            pltpu.VMEM((1, channels), jnp.float32),
            pltpu.VMEM((9 * channels, channels), bf16),
            pltpu.VMEM((1, channels), jnp.float32),
            pltpu.VMEM((channels, channels), bf16),
            pltpu.VMEM((1, channels), jnp.float32),
            pltpu.VMEM((3, extent + 2 * FIRST, extent, channels), bf16),
            pltpu.VMEM((3, extent + 2 * SECOND, extent, channels), bf16),
            pltpu.VMEM((extent, extent, channels), bf16),
            pltpu.VMEM((extent, extent, channels), bf16),
            pltpu.VMEM((extent * BLOCK, channels), jnp.float32),
            pltpu.VMEM((9 * channels, 2 * channels), bf16),
            pltpu.VMEM((2, extent * FIRST, channels), bf16),
            pltpu.VMEM((2, extent * FIRST, channels), bf16),
            pltpu.VMEM((chunks, 2, BLOCK * SECOND, channels), bf16),
            pltpu.VMEM((chunks, 2, BLOCK * SECOND, channels), bf16),
            pltpu.VMEM((side, chunks, extent // 2, BLOCK, channels), bf16),
            pltpu.VMEM((extent, extent, channels), jnp.float32),
            pltpu.SemaphoreType.DMA((9,)),
            pltpu.SemaphoreType.DMA((1 + chunks, 2)),
            pltpu.SemaphoreType.DMA((1 + chunks, 2)),
            pltpu.SemaphoreType.DMA((2, 2)),
            pltpu.SemaphoreType.DMA((2, 2)),
            pltpu.SemaphoreType.DMA((chunks,)),
            pltpu.SemaphoreType.DMA((2, chunks)),
            pltpu.SemaphoreType.DMA((chunks,)),
            pltpu.SemaphoreType.DMA((side, chunks)),
            pltpu.SemaphoreType.DMA((side, chunks)),
            pltpu.SemaphoreType.DMA((extent // 8,)),
        ],
        compiler_params=pltpu.CompilerParams(
            collective_id=0, has_side_effects=True, vmem_limit_bytes=60 * 1024 * 1024
        ),
        cost_estimate=pl.CostEstimate(
            flops=2 * cells * channels * channels * 30,
            bytes_accessed=cells * channels * 6,
            transcendentals=0,
        ),
    )(
        features,
        kernel_first.reshape(9 * channels, channels),
        bias_first.reshape(1, channels),
        mixer_first,
        shift_first.reshape(1, channels),
        kernel_second.reshape(9 * channels, channels),
        bias_second.reshape(1, channels),
        mixer_second,
        shift_second.reshape(1, channels),
    )


def solution(mesh):
    return jax.shard_map(
        body,
        mesh=mesh,
        in_specs=(P(("groups", "row"), "col", None), P(), P(), P(), P(), P(), P(), P(), P()),
        out_specs=P(("groups", "row"), "col", None),
        check_vma=False,
    )
```
